32 devices in a mesh: resp: 8 (over z, core), head: 4 (over y, x).
Axes of the slice: x: 2, y: 2, z: 4, core: 2. Of those that a mesh axis runs over, the one named last changes fastest.
Arguments:
- q_nope: bfloat16 [2048, 8192], P('resp', 'head'), may hold values from -6 to 6
- q_rope: bfloat16 [2048, 4096], P('resp', 'head'), may hold values from -160 to 160
- latents: bfloat16 [256, 576], P('resp'), may hold values from -4.1 to 4.1
- w_uk: bfloat16 [64, 128, 512], P('head'), may hold values from -0.25 to 0.25
- w_uv: bfloat16 [64, 512, 128], P('head'), may hold values from -0.25 to 0.25
- grad_out: bfloat16 [2048, 8192], P('resp', 'head'), may hold values from -6 to 6
- prompt_of: int32 [8, 4], P('resp'), may hold values from 0 to 7
- live_rows: int32 [8, 4], P('resp'), may hold values from 1 to 64, 172 in all within a row
- prompt_block: int32 [8], replicated, may hold values from 0 to 7, each once
Outputs:
- d_q_nope: bfloat16 [2048, 8192], P('resp', 'head')
- d_q_rope: bfloat16 [2048, 4096], P('resp', 'head')
- d_latents: float32 [256, 576], P('resp')
- d_w_uk: bfloat16 [64, 128, 512], P('head')
- d_w_uv: bfloat16 [64, 512, 128], P('head')
The draws below stay inside these ranges and needn't reach their ends.
Inputs may be any that keep to these rules, and one draw needn't show every extreme that they name: `live_rows`: live rows of a stretch come first; the stretches of one index of resp hold 172 live rows together, one stretch of them full. `prompt_block`: each block is named once.
All inputs are finite; a program needn't handle non-finite values.
Results may differ from the reference program's by a relative error of at most 0.0068.
Values may be sent and summed in bfloat16 or wider, within the bound.
A program may use at most 64 MiB of HBM per device.

```python
import math
import jax
import jax.numpy as jnp
import numpy as np
from jax import lax

LAT = 512
ROPE = 64
HD = 128
HEADS = 64
ROWS = 64
P_SIZE = 32
CH_DEV = 4
NPROMPT = 8
TOKENS = 2048
N_RESP = 8


def draw_latents(key, part):
    key = jax.random.fold_in(key, 11)
    values = jnp.clip(jax.random.normal(key, (NPROMPT * P_SIZE, LAT + ROPE), jnp.float32), -4.0, 4.0)
    return values.astype(jnp.bfloat16)


def draw_q_rope(key, part):
    key = jax.random.fold_in(key, 13)
    values = jnp.clip(jax.random.normal(key, (TOKENS, HEADS, ROPE), jnp.float32), -4.0, 4.0)
    return values.reshape(TOKENS, HEADS * ROPE).astype(jnp.bfloat16)


def plant(result, rng, smallest, largest):
    index_at = [jax.random.randint(jax.random.fold_in(rng, axis), (), 0, length) for axis, length in enumerate(result.shape)]
    main_axis = result.shape.index(max(result.shape))
    next_to = index_at[:main_axis] + [(index_at[main_axis] + 1) % result.shape[main_axis]] + index_at[main_axis + 1:]
    return result.at[tuple(index_at)].set(smallest).at[tuple(next_to)].set(largest)


def block_scale(rng, shape, split, low, largest):
    factor_of = 1.0
    for dim, blocks in split:
        steps = jax.random.uniform(jax.random.fold_in(jax.random.fold_in(rng, 6), dim), (blocks,), jnp.float32, low / len(split), largest / len(split))
        factor_of = factor_of * jnp.repeat(jnp.exp(steps), shape[dim] // blocks).reshape((-1,) + (1,) * (len(shape) - 1 - dim))
    return factor_of


def cumulative_ranks(amount, lean):
    portions = [(1 << 20) // math.isqrt(rank ** lean) + 1 for rank in range(1, amount + 1)]
    deviation = 1 + sum(portions) // (1 << 30)
    return np.cumsum(np.array([max(1, weight // deviation) for weight in portions]))


def ranked_ids(stream_key, extent, amount, skew):
    table = cumulative_ranks(amount, skew)
    lot = jax.random.randint(jax.random.fold_in(stream_key, 1), extent, 0, int(table[amount - 1]))
    rank = jnp.searchsorted(jnp.asarray(table, jnp.int32), lot, side="right")
    return jax.random.permutation(jax.random.fold_in(stream_key, 2), amount)[rank].astype(jnp.int32)


def profile(count, total, reach, lean):
    weights = [(1 << 20) // math.isqrt(rank ** lean) + 1 for rank in range(2, count + 1)]
    surplus, counts = total - reach - (count - 1), [1] * (count - 1)
    while surplus > 0:
        movable = [i for i in range(count - 1) if counts[i] < reach]
        mass, left = sum([weights[i] for i in movable]), surplus
        for i in movable:
            extra = min(reach - counts[i], max(1, left * weights[i] // mass), surplus)
            counts[i] = counts[i] + extra
            surplus = surplus - extra
    return np.array([reach] + counts)


def uneven(stream_key, amount, total, most, skew):
    if amount == 2:
        one = jax.random.randint(stream_key, (), max(1, total - most), min(most, total - 1) + 1)
        return jnp.stack([one, total - one])
    sizes = jnp.asarray(profile(amount, total, most, skew), jnp.int32)
    twos = (amount - 1) // 2
    giver, taker = sizes[1:1 + 2 * twos:2], sizes[2:2 + 2 * twos:2]
    room = jnp.minimum(giver - 1, most - taker)
    passed = jax.random.randint(jax.random.fold_in(stream_key, 1), (twos,), 0, 1 << 20) % (room + 1)
    sizes = sizes.at[1:1 + 2 * twos:2].set(giver - passed).at[2:2 + 2 * twos:2].set(taker + passed)
    return sizes[jax.random.permutation(jax.random.fold_in(stream_key, 2), amount)]


def bell_draw(key, shape, scale, limit, split=(), held_as=jnp.bfloat16):
    result = scale * jax.random.normal(key, shape, jnp.float32)
    if split:
        result = result * block_scale(key, shape, split, -0.22, 0.18)
    return jnp.clip(result, -limit, limit).astype(held_as)


def setup_inputs(seed: int = 0) -> dict:
    splits = jax.random.split(jax.random.key(seed), 10)
    q_nope = bell_draw(splits[0], (TOKENS, HEADS * HD), 1.0, 6.0, ((0, 8), (1, 4)))
    q_rope = draw_q_rope(jax.random.fold_in(splits[9], 71), 0)
    latents = draw_latents(jax.random.fold_in(splits[9], 71), 0)
    w_uk = bell_draw(splits[3], (HEADS, HD, LAT), LAT ** -0.5, 0.25, ((0, 4),))
    w_uv = bell_draw(splits[4], (HEADS, LAT, HD), LAT ** -0.5, 0.25, ((0, 4),))
    grad_out = bell_draw(splits[5], (TOKENS, HEADS * HD), 1.0, 6.0, ((0, 8), (1, 4)))
    prompt_of = plant(ranked_ids(splits[6], (N_RESP, CH_DEV), NPROMPT, 2), jax.random.fold_in(splits[6], 3), 0, NPROMPT - 1).astype(jnp.int32)
    live_rows = jax.vmap(lambda own: uneven(own, CH_DEV, ROWS + (CH_DEV - 1) * ROWS * 9 // 16, ROWS, 2))(jax.random.split(splits[7], N_RESP)).reshape((N_RESP, CH_DEV)).astype(jnp.int32)
    prompt_block = jax.random.permutation(splits[8], NPROMPT).astype(jnp.int32)
    return {"q_nope": q_nope, "q_rope": q_rope, "latents": latents, "w_uk": w_uk, "w_uv": w_uv, "grad_out": grad_out, "prompt_of": prompt_of, "live_rows": live_rows, "prompt_block": prompt_block}


def rounded(value):
    return lax.optimization_barrier(value.astype(jnp.bfloat16)).astype(jnp.float32)


def reference(q_nope, q_rope, latents, w_uk, w_uv, grad_out, prompt_of, live_rows, prompt_block):
    scale = (HD + ROPE) ** -0.5
    stretches = N_RESP * CH_DEV
    flat_prompt = prompt_of.reshape(stretches).astype(jnp.int32)
    flat_live = live_rows.reshape(stretches).astype(jnp.int32)
    query_nope = q_nope.reshape(stretches, ROWS, HEADS, HD)
    query_rope = q_rope.reshape(stretches, ROWS, HEADS, ROPE)
    cotangent = grad_out.reshape(stretches, ROWS, HEADS, HD)
    key_up = w_uk.astype(jnp.float32)
    value_up = w_uv.astype(jnp.float32)

    def step(carry, item):
        grad_uk, grad_uv, grad_lat = carry
        qn_stretch, qr_stretch, go_stretch, prompt, live = item
        start = (prompt_block[prompt] * P_SIZE).astype(jnp.int32)
        keys = lax.dynamic_slice_in_dim(latents, start, P_SIZE, 0).astype(jnp.float32)
        latent_part = keys[:, :LAT]
        mask = jnp.arange(ROWS, dtype=jnp.int32) < live
        grad_rows = jnp.where(mask[:, None, None], go_stretch.astype(jnp.float32), 0.0)
        qn_float = qn_stretch.astype(jnp.float32)
        q_abs = rounded(jnp.einsum('rhd,hdl->rhl', qn_float, key_up))
        q_cat = jnp.concatenate([q_abs, qr_stretch.astype(jnp.float32)], axis=-1)
        scores = jnp.einsum('rhk,pk->hrp', q_cat, keys) * scale
        probs = jax.nn.softmax(scores, axis=-1)
        probs_low = rounded(probs)
        out_lat = rounded(jnp.einsum('hrp,pl->rhl', probs_low, latent_part))
        d_out = rounded(jnp.einsum('rhd,hld->rhl', grad_rows, value_up))
        grad_uv = grad_uv + jnp.einsum('rhl,rhd->hld', out_lat, grad_rows)
        d_probs = jnp.einsum('rhl,pl->hrp', d_out, latent_part)
        delta = jnp.sum(probs * d_probs, axis=-1, keepdims=True)
        d_scores = rounded(probs * (d_probs - delta))
        d_full = jnp.einsum('hrp,pk->rhk', d_scores, keys) * scale
        d_abs = rounded(d_full[..., :LAT])
        d_rope = d_full[..., LAT:].astype(jnp.bfloat16)
        d_keys = jnp.einsum('hrp,rhk->pk', d_scores, q_cat) * scale
        d_vals = jnp.einsum('hrp,rhl->pl', probs_low, d_out)
        d_keys = d_keys + jnp.pad(d_vals, ((0, 0), (0, ROPE)))
        old = lax.dynamic_slice_in_dim(grad_lat, start, P_SIZE, 0)
        grad_lat = lax.dynamic_update_slice_in_dim(grad_lat, old + d_keys, start, 0)
        d_nope = jnp.einsum('rhl,hdl->rhd', d_abs, key_up).astype(jnp.bfloat16)
        grad_uk = grad_uk + jnp.einsum('rhd,rhl->hdl', qn_float, d_abs)
        return (grad_uk, grad_uv, grad_lat), (d_nope, d_rope)

    init = (jnp.zeros((HEADS, HD, LAT), jnp.float32), jnp.zeros((HEADS, LAT, HD), jnp.float32),
            jnp.zeros((NPROMPT * P_SIZE, LAT + ROPE), jnp.float32))
    carry, stacked = lax.scan(step, init, (query_nope, query_rope, cotangent, flat_prompt, flat_live))
    grad_uk, grad_uv, grad_lat = carry
    d_nope, d_rope = stacked
    return (d_nope.reshape(TOKENS, HEADS * HD), d_rope.reshape(TOKENS, HEADS * ROPE), grad_lat,
            grad_uk.astype(jnp.bfloat16), grad_uv.astype(jnp.bfloat16))
```

```python
import functools

import jax
import jax.numpy as jnp
from jax import lax
from jax.experimental import pallas as pl
from jax.experimental.pallas import tpu as pltpu
from jax.sharding import PartitionSpec as P

LAT = 512
ROPE = 64
HD = 128
ROWS = 64
P_SIZE = 32
SCALE = (HD + ROPE) ** (-0.5)
BF = jnp.bfloat16
F32 = jnp.float32


def dot_nn(a, b):
    return lax.dot_general(a, b, (((1,), (0,)), ((), ())), preferred_element_type=F32)


def dot_nt(a, b):
    return lax.dot_general(a, b, (((1,), (1,)), ((), ())), preferred_element_type=F32)


def dot_tn(a, b):
    return lax.dot_general(a, b, (((0,), (0,)), ((), ())), preferred_element_type=F32)


def local_kernel(
    live_ref, qn_ref, qr_ref, go_ref, wk_ref, wv_ref, lat_ref, rope_ref,
    dqn_ref, dqr_ref, dkv_ref, dc_ref, dr_ref,
):
    tokens = qn_ref.shape[0]
    keys = lat_ref.shape[0]
    stretches = keys // P_SIZE
    row = lax.broadcasted_iota(jnp.int32, (tokens, keys), 0)
    lane = lax.broadcasted_iota(jnp.int32, (tokens, keys), 1)
    own = (row // ROWS) == (lane // P_SIZE)
    row_h = lax.broadcasted_iota(jnp.int32, (tokens, HD), 0)
    limit = jnp.zeros((tokens, HD), jnp.int32)
    for c in range(stretches):
        limit = jnp.where(row_h // ROWS == c, live_ref[c], limit)
    live = (row_h % ROWS) < limit
    lat = lat_ref[...]
    qr = qr_ref[...]
    dqr = jnp.zeros((tokens, 2 * ROPE), F32)
    dc = jnp.zeros((keys, LAT), F32)

    @pl.when(pl.program_id(0) == 0)
    def _():
        dc_ref[...] = jnp.zeros_like(dc_ref)
        dr_ref[...] = jnp.zeros_like(dr_ref)

    for i in range(2):
        cols = slice(i * HD, (i + 1) * HD)
        qn = qn_ref[:, cols]
        g = jnp.where(live, go_ref[:, cols], jnp.zeros((), BF))
        kn = dot_nt(lat, wk_ref[i]).astype(BF)
        vn = dot_nn(lat, wv_ref[i]).astype(BF)
        rope = rope_ref[i]
        s = dot_nt(
            jnp.concatenate([qn, qr], axis=1), jnp.concatenate([kn, rope], axis=1)
        ) * SCALE
        s = jnp.where(own, s, -jnp.inf)
        e = jnp.exp(s - jnp.max(s, axis=1, keepdims=True))
        p = e / jnp.sum(e, axis=1, keepdims=True)
        pb = p.astype(BF)
        dp = dot_nt(g, vn)
        delta = jnp.sum(p * dp, axis=1, keepdims=True)
        ds = (p * (dp - delta)).astype(BF)
        dqn_ref[:, cols] = (dot_nn(ds, kn) * SCALE).astype(BF)
        dqr = dqr + dot_nn(ds, rope)
        dk = (dot_tn(ds, qn) * SCALE).astype(BF)
        dv = dot_tn(pb, g).astype(BF)
        dkv_ref[2 * i] = dk
        dkv_ref[2 * i + 1] = dv
        dc = dc + dot_nn(dk, wk_ref[i]) + dot_nt(dv, wv_ref[i])
        dr_ref[i] += dot_tn(ds, qr) * SCALE
    dqr_ref[...] = (dqr * SCALE).astype(BF)
    dc_ref[...] += dc


def local_part(live, qn, qr, go, wk, wv, lat, rope2):
    heads = wk.shape[0]
    tokens = qn.shape[0]
    keys = lat.shape[0]
    full = lambda *shape: pl.BlockSpec(shape, lambda i: (0,) * len(shape))
    return pl.pallas_call(
        local_kernel,
        grid=(heads // 2,),
        in_specs=[
            pl.BlockSpec(memory_space=pltpu.SMEM),
            pl.BlockSpec((tokens, 2 * HD), lambda i: (0, i)),
            pl.BlockSpec((tokens, 2 * ROPE), lambda i: (0, i)),
            pl.BlockSpec((tokens, 2 * HD), lambda i: (0, i)),
            pl.BlockSpec((2, HD, LAT), lambda i: (i, 0, 0)),
            pl.BlockSpec((2, LAT, HD), lambda i: (i, 0, 0)),
            full(keys, LAT),
            full(2, keys, 2 * ROPE),
        ],
        out_specs=[
            pl.BlockSpec((tokens, 2 * HD), lambda i: (0, i)),
            pl.BlockSpec((tokens, 2 * ROPE), lambda i: (0, i)),
            pl.BlockSpec((4, keys, HD), lambda i: (i, 0, 0)),
            full(keys, LAT),
            full(2, keys, 2 * ROPE),
        ],
        out_shape=[
            jax.ShapeDtypeStruct((tokens, heads * HD), BF),
            jax.ShapeDtypeStruct((tokens, heads * ROPE), BF),
            jax.ShapeDtypeStruct((2 * heads, keys, HD), BF),
            jax.ShapeDtypeStruct((keys, LAT), F32),
            jax.ShapeDtypeStruct((2, keys, 2 * ROPE), F32),
        ],
        compiler_params=pltpu.CompilerParams(vmem_limit_bytes=32 * 2**20),
    )(live, qn, qr, go, wk, wv, lat, rope2)


def per_device(q_nope, q_rope, latents, w_uk, w_uv, grad_out, prompt_of, live_rows, prompt_block):
    heads = w_uk.shape[0]
    gathered = lax.all_gather(latents, "resp", axis=0, tiled=True)
    rows = gathered.shape[0]
    blocks = prompt_block[prompt_of[0]]
    keys = jnp.take(
        gathered.reshape(rows // P_SIZE, P_SIZE, LAT + ROPE), blocks, axis=0
    ).reshape(-1, LAT + ROPE)
    rope = keys[:, LAT:]
    none = jnp.zeros_like(rope)
    rope2 = jnp.stack(
        [jnp.concatenate([rope, none], axis=1), jnp.concatenate([none, rope], axis=1)]
    )
    d_nope, d_rope, dkv, dc, dr = local_part(
        live_rows[0], q_nope, q_rope, grad_out, w_uk, w_uv, keys[:, :LAT], rope2
    )
    row_of = (blocks[:, None] * P_SIZE + jnp.arange(P_SIZE)[None, :]).reshape(-1)
    select = jnp.arange(rows)[:, None] == row_of[None, :]
    d_keys = jnp.concatenate([dc, dr[0, :, :ROPE] + dr[1, :, ROPE:]], axis=1)
    partial_rows = jnp.dot(select.astype(F32), d_keys, precision=lax.Precision.HIGHEST)
    holder_rows = lax.psum_scatter(partial_rows, "resp", scatter_dimension=0, tiled=True)
    grad_lat = lax.psum(holder_rows, "head")
    spread = jnp.einsum("nk,ukd->und", select.astype(BF), dkv, preferred_element_type=F32)
    summed = lax.psum(spread.astype(BF), "resp").reshape(heads, 2, rows, HD)
    lat_all = gathered[:, :LAT]
    final_uk = jnp.einsum("hnd,nl->hdl", summed[:, 0], lat_all, preferred_element_type=F32)
    final_uv = jnp.einsum("nl,hnd->hld", lat_all, summed[:, 1], preferred_element_type=F32)
    return d_nope, d_rope, grad_lat, final_uk.astype(BF), final_uv.astype(BF)


def solution(mesh):
    in_specs = (
        P("resp", "head"),
        P("resp", "head"),
        P("resp", None),
        P("head", None, None),
        P("head", None, None),
        P("resp", "head"),
        P("resp", None),
        P("resp", None),
        P(),
    )
    out_specs = (
        P("resp", "head"),
        P("resp", "head"),
        P("resp", None),
        P("head", None, None),
        P("head", None, None),
    )
    return jax.shard_map(
        per_device, mesh=mesh, in_specs=in_specs, out_specs=out_specs, check_vma=False
    )
```

```python
import functools

import jax
import jax.numpy as jnp
from jax import lax
from jax.experimental import pallas as pl
from jax.experimental.pallas import tpu as pltpu
from jax.sharding import PartitionSpec as P

LAT = 512
ROPE = 64
HD = 128
ROWS = 64
P_SIZE = 32
SCALE = (HD + ROPE) ** (-0.5)
BF = jnp.bfloat16
F32 = jnp.float32


def dot_nn(a, b):
    return lax.dot_general(a, b, (((1,), (0,)), ((), ())), preferred_element_type=F32)


def dot_nt(a, b):
    return lax.dot_general(a, b, (((1,), (1,)), ((), ())), preferred_element_type=F32)


def dot_tn(a, b):
    return lax.dot_general(a, b, (((0,), (0,)), ((), ())), preferred_element_type=F32)


def local_kernel(
    live_ref, qn_ref, qr_ref, go_ref, wk_ref, wv_ref, lat_ref, rope_ref,
    dqn_ref, dqr_ref, dkv_ref, dc_ref, dr_ref,
):
    tokens = qn_ref.shape[0]
    keys = lat_ref.shape[0]
    stretches = keys // P_SIZE
    row = lax.broadcasted_iota(jnp.int32, (tokens, keys), 0)
    lane = lax.broadcasted_iota(jnp.int32, (tokens, keys), 1)
    own = (row // ROWS) == (lane // P_SIZE)
    row_h = lax.broadcasted_iota(jnp.int32, (tokens, HD), 0)
    limit = jnp.zeros((tokens, HD), jnp.int32)
    for c in range(stretches):
        limit = jnp.where(row_h // ROWS == c, live_ref[c], limit)
    live = (row_h % ROWS) < limit
    lat = lat_ref[...]
    qr = qr_ref[...]
    dqr = jnp.zeros((tokens, 2 * ROPE), F32)
    dc = jnp.zeros((keys, LAT), F32)

    @pl.when(pl.program_id(0) == 0)
    def _():
        dc_ref[...] = jnp.zeros_like(dc_ref)
        dr_ref[...] = jnp.zeros_like(dr_ref)

    for i in range(2):
        cols = slice(i * HD, (i + 1) * HD)
        qn = qn_ref[:, cols]
        g = jnp.where(live, go_ref[:, cols], jnp.zeros((), BF))
        kn = dot_nt(lat, wk_ref[i]).astype(BF)
        vn = dot_nn(lat, wv_ref[i]).astype(BF)
        rope = rope_ref[i]
        s = dot_nt(
            jnp.concatenate([qn, qr], axis=1), jnp.concatenate([kn, rope], axis=1)
        ) * SCALE
        s = jnp.where(own, s, -jnp.inf)
        e = jnp.exp(s - jnp.max(s, axis=1, keepdims=True))
        p = e / jnp.sum(e, axis=1, keepdims=True)
        pb = p.astype(BF)
        dp = dot_nt(g, vn)
        delta = jnp.sum(p * dp, axis=1, keepdims=True)
        ds = (p * (dp - delta)).astype(BF)
        dqn_ref[:, cols] = (dot_nn(ds, kn) * SCALE).astype(BF)
        dqr = dqr + dot_nn(ds, rope)
        dk = (dot_tn(ds, qn) * SCALE).astype(BF)
        dv = dot_tn(pb, g).astype(BF)
        dkv_ref[0, :, 2 * i * HD:(2 * i + 1) * HD] = dk
        dkv_ref[0, :, (2 * i + 1) * HD:(2 * i + 2) * HD] = dv
        dc = dc + dot_nn(dk, wk_ref[i]) + dot_nt(dv, wv_ref[i])
        dr_ref[i] += dot_tn(ds, qr) * SCALE
    dqr_ref[...] = (dqr * SCALE).astype(BF)
    dc_ref[...] += dc


def local_part(live, qn, qr, go, wk, wv, lat, rope2):
    heads = wk.shape[0]
    tokens = qn.shape[0]
    keys = lat.shape[0]
    full = lambda *shape: pl.BlockSpec(shape, lambda i: (0,) * len(shape))
    return pl.pallas_call(
        local_kernel,
        grid=(heads // 2,),
        in_specs=[
            pl.BlockSpec(memory_space=pltpu.SMEM),
            pl.BlockSpec((tokens, 2 * HD), lambda i: (0, i)),
            pl.BlockSpec((tokens, 2 * ROPE), lambda i: (0, i)),
            pl.BlockSpec((tokens, 2 * HD), lambda i: (0, i)),
            pl.BlockSpec((2, HD, LAT), lambda i: (i, 0, 0)),
            pl.BlockSpec((2, LAT, HD), lambda i: (i, 0, 0)),
            full(keys, LAT),
            full(2, keys, 2 * ROPE),
        ],
        out_specs=[
            pl.BlockSpec((tokens, 2 * HD), lambda i: (0, i)),
            pl.BlockSpec((tokens, 2 * ROPE), lambda i: (0, i)),
            pl.BlockSpec((1, keys, 4 * HD), lambda i: (i, 0, 0)),
            full(keys, LAT),
            full(2, keys, 2 * ROPE),
        ],
        out_shape=[
            jax.ShapeDtypeStruct((tokens, heads * HD), BF),
            jax.ShapeDtypeStruct((tokens, heads * ROPE), BF),
            jax.ShapeDtypeStruct((heads // 2, keys, 4 * HD), BF),
            jax.ShapeDtypeStruct((keys, LAT), F32),
            jax.ShapeDtypeStruct((2, keys, 2 * ROPE), F32),
        ],
        compiler_params=pltpu.CompilerParams(vmem_limit_bytes=32 * 2**20),
    )(live, qn, qr, go, wk, wv, lat, rope2)


MESH = pl.DeviceIdType.MESH
ID_ROWS = 16


def at_resp(r):
    return (r, lax.axis_index("head"))


def greet(peers):
    barrier = pltpu.get_barrier_semaphore()
    for peer in peers:
        pl.semaphore_signal(barrier, inc=1, device_id=peer, device_id_type=MESH)
    pl.semaphore_wait(barrier, len(peers))


def spread_blocks(n, me, buf, send, near, far, passed):
    sibling = me + 1 - 2 * lax.rem(me, 2)

    def copy(slot, to, s, recv):
        return pltpu.make_async_remote_copy(
            src_ref=buf.at[slot], dst_ref=buf.at[slot], send_sem=send.at[s], recv_sem=recv,
            device_id=at_resp(to), device_id_type=MESH,
        )

    hops = n // 2
    out = [copy(me, lax.rem(me + 2 * k, n), k, far.at[k]) for k in range(1, hops)]
    own = copy(me, sibling, 0, near.at[0])
    for c in out:
        c.start()
    own.start()
    handed = []
    for k in range(1, hops):
        out[k - 1].wait_recv()
        c = copy(lax.rem(me - 2 * k + n, n), sibling, hops + k - 1, passed.at[k])
        c.start()
        handed.append(c)
    own.wait()
    for c in out:
        c.wait_send()
    for c in handed:
        c.wait()


def gather_kernel(n, mine_ref, all_ref, send, near, far, passed):
    me = lax.axis_index("resp")
    sibling = me + 1 - 2 * lax.rem(me, 2)
    greet([at_resp(lax.rem(me + 2 * k, n)) for k in range(1, n // 2)] + [at_resp(sibling)])
    all_ref[me] = mine_ref[...]
    spread_blocks(n, me, all_ref, send, near, far, passed)


def spread_scratch(n):
    return [
        pltpu.SemaphoreType.DMA((n,)),
        pltpu.SemaphoreType.DMA((1,)),
        pltpu.SemaphoreType.DMA((n // 2,)),
        pltpu.SemaphoreType.DMA((n // 2,)),
    ]


VM = pl.BlockSpec(memory_space=pltpu.VMEM)


def gather_blocks(n, mine):
    return pl.pallas_call(
        functools.partial(gather_kernel, n),
        out_shape=jax.ShapeDtypeStruct((n,) + mine.shape, mine.dtype),
        in_specs=[VM],
        out_specs=VM,
        scratch_shapes=spread_scratch(n),
        compiler_params=pltpu.CompilerParams(
            collective_id=1, has_side_effects=True, vmem_limit_bytes=6 * 2**20
        ),
    )(mine)


CHIPS = 4
PARTS = 8


def sum_kernel(
    n, nh, dkv_ref, rows_ref, sel_ref, all_ref, lat_ref,
    got_rows, at_head, sib, mine, outer, half, other,
    s2, r2, s3, r3, ss, sr, es, er, hs, hr, ts, tr, gs, gr,
):
    me = lax.axis_index("resp")
    head = lax.axis_index("head")
    core = lax.rem(me, 2)
    z = me // 2
    sibling = me + 1 - 2 * core
    beside = 2 * (z + 1 - 2 * lax.rem(z, 2)) + core
    across = 2 * (CHIPS - 1 - z) + core
    inner = (z == 1) | (z == 2)
    peers = [lax.rem(me + k, n) for k in range(1, n)]
    heads = [lax.rem(head + k, nh) for k in range(1, nh)]
    greet([at_resp(r) for r in peers] + [(me, h) for h in heads])
    pairs = dkv_ref.shape[0] // 2
    keys = mine.shape[1]

    def copy(src, dst, s, r, i, to):
        return pltpu.make_async_remote_copy(
            src_ref=src, dst_ref=dst, send_sem=s.at[i], recv_sem=r.at[i],
            device_id=to, device_id_type=MESH,
        )

    sib_copies = [
        copy(dkv_ref.at[(1 - core) * pairs + j], sib.at[j], ss, sr, j, at_resp(sibling))
        for j in range(pairs)
    ]
    for c in sib_copies:
        c.start()
    row_copies = [
        copy(rows_ref.at[peers[k]], got_rows.at[k], s2, r2, k, at_resp(peers[k])) for k in range(n - 1)
    ]
    for c in row_copies:
        c.start()
    head_copies = [
        copy(at_head.at[head], at_head.at[head], s3, r3, k, (me, heads[k])) for k in range(nh - 1)
    ]
    inwards = [copy(mine.at[i], outer.at[i], es, er, i, at_resp(beside)) for i in range(PARTS)]
    middle = [copy(half.at[i], other.at[i], hs, hr, i, at_resp(across)) for i in range(PARTS)]
    slots = [all_ref.at[core * PARTS + i] for i in range(PARTS)]
    outwards = [copy(slots[i], slots[i], ts, tr, i, at_resp(beside)) for i in range(PARTS)]
    shared = [copy(slots[i], slots[i], gs, gr, i, at_resp(sibling)) for i in range(PARTS)]

    def chip_terms(j):
        sib_copies[j].wait_recv()
        total = dot_nn(sel_ref[me], dkv_ref[core * pairs + j]) + dot_nn(sel_ref[sibling], sib[j])
        mine[2 * j] = total[:keys].astype(BF)
        mine[2 * j + 1] = total[keys:].astype(BF)

    def sum_rows():
        rows = rows_ref[me].astype(F32)
        for k in range(n - 1):
            row_copies[k].wait_recv()
            rows = rows + got_rows[k].astype(F32)
        at_head[head] = rows
        for c in head_copies:
            c.start()

    def finish(i):
        middle[i].wait_recv()
        all_ref[core * PARTS + i] = (half[i].astype(F32) + other[i].astype(F32)).astype(BF)
        outwards[i].start()
        shared[i].start()

    @pl.when(inner)
    def _():
        for j in range(pairs):
            chip_terms(j)
        for i in range(PARTS):
            inwards[i].wait_recv()
            half[i] = (mine[i].astype(F32) + outer[i].astype(F32)).astype(BF)
            middle[i].start()
            if i >= 1:
                finish(i - 1)
            if i == PARTS // 2:
                sum_rows()
        finish(PARTS - 1)
        for i in range(PARTS):
            middle[i].wait_send()
            outwards[i].wait_send()

    @pl.when(jnp.logical_not(inner))
    def _():
        for j in range(pairs):
            chip_terms(j)
            inwards[2 * j].start()
            inwards[2 * j + 1].start()
        sum_rows()
        for i in range(PARTS):
            outwards[i].wait_recv()
            shared[i].start()
        for i in range(PARTS):
            inwards[i].wait_send()

    for c in head_copies:
        c.wait()
    lat = at_head[0]
    for h in range(1, nh):
        lat = lat + at_head[h]
    lat_ref[...] = lat
    for c in shared:
        c.wait()
    for c in row_copies + sib_copies:
        c.wait_send()


def sum_parts(n, nh, dkv, rows, select):
    pairs, keys, wide = dkv.shape
    dma = lambda k: pltpu.SemaphoreType.DMA((k,))
    part = pltpu.VMEM((PARTS, select.shape[1] // 2, wide), BF)
    summed, lat = pl.pallas_call(
        functools.partial(sum_kernel, n, nh),
        out_shape=[
            jax.ShapeDtypeStruct((2 * pairs, select.shape[1] // 2, wide), BF),
            jax.ShapeDtypeStruct(rows.shape[1:], F32),
        ],
        in_specs=[VM] * 3,
        out_specs=[VM] * 2,
        scratch_shapes=[
            pltpu.VMEM((n - 1,) + rows.shape[1:], BF),
            pltpu.VMEM((nh,) + rows.shape[1:], F32),
            pltpu.VMEM((pairs // 2, keys, wide), BF),
            part, part, part, part,
            dma(n - 1), dma(n - 1), dma(nh - 1), dma(nh - 1), dma(pairs // 2), dma(pairs // 2),
        ] + [dma(PARTS)] * 8,
        compiler_params=pltpu.CompilerParams(
            collective_id=2, has_side_effects=True, vmem_limit_bytes=32 * 2**20
        ),
    )(dkv, rows, select)
    return summed.reshape(pairs, select.shape[1], wide), lat


def weights_kernel(sum_ref, lat_ref, duk_ref, duv_ref):
    lat = lat_ref[...]
    for i in range(2):
        at = 2 * i * HD
        duk_ref[i] = dot_tn(sum_ref[0, :, at:at + HD], lat).astype(BF)
        duv_ref[i] = dot_tn(lat, sum_ref[0, :, at + HD:at + 2 * HD]).astype(BF)


def weight_grads(summed, lat_all):
    pairs, rows, wide = summed.shape
    return pl.pallas_call(
        weights_kernel,
        grid=(pairs,),
        in_specs=[
            pl.BlockSpec((1, rows, wide), lambda i: (i, 0, 0)),
            pl.BlockSpec((rows, LAT), lambda i: (0, 0)),
        ],
        out_specs=[
            pl.BlockSpec((2, HD, LAT), lambda i: (i, 0, 0)),
            pl.BlockSpec((2, LAT, HD), lambda i: (i, 0, 0)),
        ],
        out_shape=[
            jax.ShapeDtypeStruct((2 * pairs, HD, LAT), BF),
            jax.ShapeDtypeStruct((2 * pairs, LAT, HD), BF),
        ],
        compiler_params=pltpu.CompilerParams(vmem_limit_bytes=32 * 2**20),
    )(summed, lat_all)


def per_device(
    n, nh, q_nope, q_rope, latents, w_uk, w_uv, grad_out, prompt_of, live_rows, prompt_block
):
    pairs = w_uk.shape[0] // 2
    held = latents.shape[0]
    stretches = prompt_of.shape[1]
    blocks = prompt_block[prompt_of[0]]
    ids = jnp.zeros((ID_ROWS, LAT + ROPE), BF).at[0, :stretches].set(blocks.astype(BF))
    gathered = gather_blocks(n, jnp.concatenate([latents, ids], axis=0))
    table = gathered[:, :held].reshape(n * held, LAT + ROPE)
    all_blocks = gathered[:, held, :stretches].astype(jnp.int32)
    rows = n * held
    keys = jnp.take(
        table.reshape(rows // P_SIZE, P_SIZE, LAT + ROPE), blocks, axis=0
    ).reshape(-1, LAT + ROPE)
    rope = keys[:, LAT:]
    none = jnp.zeros_like(rope)
    rope2 = jnp.stack(
        [jnp.concatenate([rope, none], axis=1), jnp.concatenate([none, rope], axis=1)]
    )
    d_nope, d_rope, dkv, dc, dr = local_part(
        live_rows[0], q_nope, q_rope, grad_out, w_uk, w_uv, keys[:, :LAT], rope2
    )

    def rows_of(which):
        at = which[..., :, None] * P_SIZE + jnp.arange(P_SIZE)
        at = at.reshape(which.shape[:-1] + (-1,))
        return jnp.arange(rows)[:, None] == at[..., None, :]

    d_keys = jnp.concatenate([dc, dr[0, :, :ROPE] + dr[1, :, ROPE:]], axis=1)
    select = rows_of(blocks)
    partial_rows = jnp.dot(select.astype(F32), d_keys, precision=lax.Precision.HIGHEST)
    if pairs == n == 2 * CHIPS:
        summed, grad_lat = sum_parts(
            n, nh, dkv, partial_rows.astype(BF).reshape(n, held, LAT + ROPE),
            rows_of(all_blocks).astype(BF),
        )
    else:
        holder_rows = lax.psum_scatter(partial_rows, "resp", scatter_dimension=0, tiled=True)
        grad_lat = lax.psum(holder_rows, "head")
        spread = jnp.einsum("nk,ukd->und", select.astype(BF), dkv, preferred_element_type=F32)
        summed = lax.psum(spread, "resp").astype(BF)
    final_uk, final_uv = weight_grads(summed, table[:, :LAT])
    return d_nope, d_rope, grad_lat, final_uk, final_uv


def solution(mesh):
    in_specs = (
        P("resp", "head"),
        P("resp", "head"),
        P("resp", None),
        P("head", None, None),
        P("head", None, None),
        P("resp", "head"),
        P("resp", None),
        P("resp", None),
        P(),
    )
    out_specs = (
        P("resp", "head"),
        P("resp", "head"),
        P("resp", None),
        P("head", None, None),
        P("head", None, None),
    )
    return jax.shard_map(
        functools.partial(per_device, mesh.shape["resp"], mesh.shape["head"]), mesh=mesh, in_specs=in_specs, out_specs=out_specs, check_vma=False
    )
```

```python
import functools

import jax
import jax.numpy as jnp
from jax import lax
from jax.experimental import pallas as pl
from jax.experimental.pallas import tpu as pltpu
from jax.sharding import PartitionSpec as P

LAT = 512
ROPE = 64
HD = 128
ROWS = 64
P_SIZE = 32
SCALE = (HD + ROPE) ** (-0.5)
BF = jnp.bfloat16
F32 = jnp.float32
STEP = 4


def dot_nn(a, b):
    return lax.dot_general(a, b, (((1,), (0,)), ((), ())), preferred_element_type=F32)


def dot_nt(a, b):
    return lax.dot_general(a, b, (((1,), (1,)), ((), ())), preferred_element_type=F32)


def dot_tn(a, b):
    return lax.dot_general(a, b, (((0,), (0,)), ((), ())), preferred_element_type=F32)


def local_kernel(
    live_ref, qn_ref, qr_ref, go_ref, wk_ref, wv_ref, keys_ref,
    dqn_ref, dqr_ref, dkv_ref, dkeys_ref, dc_ref, dr_ref,
):
    tokens = qn_ref.shape[0]
    keys = keys_ref.shape[0]
    stretches = keys // P_SIZE
    row = lax.broadcasted_iota(jnp.int32, (tokens, keys), 0)
    lane = lax.broadcasted_iota(jnp.int32, (tokens, keys), 1)
    own = (row // ROWS) == (lane // P_SIZE)
    row_h = lax.broadcasted_iota(jnp.int32, (tokens, HD), 0)
    limit = jnp.zeros((tokens, HD), jnp.int32)
    for c in range(stretches):
        limit = jnp.where(row_h // ROWS == c, live_ref[c], limit)
    live = (row_h % ROWS) < limit
    lat = keys_ref[:, :LAT]
    rope = keys_ref[:, LAT:]
    none = jnp.zeros_like(rope)
    ropes = [jnp.concatenate([rope, none], axis=1), jnp.concatenate([none, rope], axis=1)]
    dc = jnp.zeros((keys, LAT), F32)

    @pl.when(pl.program_id(0) == 0)
    def _():
        dc_ref[...] = jnp.zeros_like(dc_ref)
        dr_ref[...] = jnp.zeros_like(dr_ref)

    for pair in range(STEP // 2):
        rope_cols = slice(2 * pair * ROPE, 2 * (pair + 1) * ROPE)
        qr = qr_ref[:, rope_cols]
        dqr = jnp.zeros((tokens, 2 * ROPE), F32)
        for i in range(2):
            at = 2 * pair + i
            cols = slice(at * HD, (at + 1) * HD)
            g = jnp.where(live, go_ref[:, cols], jnp.zeros((), BF))
            kn = dot_nt(lat, wk_ref[at]).astype(BF)
            vn = dot_nn(lat, wv_ref[at]).astype(BF)
            q_all = jnp.concatenate([qn_ref[:, cols], qr], axis=1)
            k_all = jnp.concatenate([kn, ropes[i]], axis=1)
            s = jnp.where(own, dot_nt(q_all, k_all) * SCALE, -jnp.inf)
            e = jnp.exp(s - jnp.max(s, axis=1, keepdims=True))
            p = e * (1.0 / jnp.sum(e, axis=1, keepdims=True))
            dp = dot_nt(g, vn)
            delta = jnp.sum(p * dp, axis=1, keepdims=True)
            ds = (p * (dp - delta)).astype(BF)
            dq = dot_nn(ds, k_all) * SCALE
            dqn_ref[:, cols] = dq[:, :HD].astype(BF)
            dqr = dqr + dq[:, HD:]
            dk_all = dot_tn(ds, q_all) * SCALE
            dk = dk_all[:, :HD].astype(BF)
            dv = dot_tn(p.astype(BF), g).astype(BF)
            dkv_ref[pair, :, 2 * i * HD:(2 * i + 1) * HD] = dk
            dkv_ref[pair, :, (2 * i + 1) * HD:(2 * i + 2) * HD] = dv
            dc = dc + dot_nn(dk, wk_ref[at]) + dot_nt(dv, wv_ref[at])
            dr_ref[i] += dk_all[:, HD:]
        dqr_ref[:, rope_cols] = dqr.astype(BF)
    dc_ref[...] += dc

    @pl.when(pl.program_id(0) == pl.num_programs(0) - 1)
    def _():
        dkeys_ref[:, :LAT] = dc_ref[...]
        dkeys_ref[:, LAT:] = dr_ref[0][:, :ROPE] + dr_ref[1][:, ROPE:]


def local_part(live, qn, qr, go, wk, wv, k_rows):
    heads = wk.shape[0]
    tokens = qn.shape[0]
    keys = k_rows.shape[0]
    full = lambda *shape: pl.BlockSpec(shape, lambda i: (0,) * len(shape))
    return pl.pallas_call(
        local_kernel,
        grid=(heads // STEP,),
        in_specs=[
            pl.BlockSpec(memory_space=pltpu.SMEM),
            pl.BlockSpec((tokens, STEP * HD), lambda i: (0, i)),
            pl.BlockSpec((tokens, STEP * ROPE), lambda i: (0, i)),
            pl.BlockSpec((tokens, STEP * HD), lambda i: (0, i)),
            pl.BlockSpec((STEP, HD, LAT), lambda i: (i, 0, 0)),
            pl.BlockSpec((STEP, LAT, HD), lambda i: (i, 0, 0)),
            full(keys, LAT + ROPE),
        ],
        out_specs=[
            pl.BlockSpec((tokens, STEP * HD), lambda i: (0, i)),
            pl.BlockSpec((tokens, STEP * ROPE), lambda i: (0, i)),
            pl.BlockSpec((STEP // 2, keys, 4 * HD), lambda i: (i, 0, 0)),
            full(keys, LAT + ROPE),
        ],
        out_shape=[
            jax.ShapeDtypeStruct((tokens, heads * HD), BF),
            jax.ShapeDtypeStruct((tokens, heads * ROPE), BF),
            jax.ShapeDtypeStruct((heads // 2, keys, 4 * HD), BF),
            jax.ShapeDtypeStruct((keys, LAT + ROPE), F32),
        ],
        scratch_shapes=[pltpu.VMEM((keys, LAT), F32), pltpu.VMEM((2, keys, 2 * ROPE), F32)],
        compiler_params=pltpu.CompilerParams(vmem_limit_bytes=60 * 2**20),
    )(live, qn, qr, go, wk, wv, k_rows)


MESH = pl.DeviceIdType.MESH
ID_ROWS = 16


def at_resp(r):
    return (r, lax.axis_index("head"))


def greet(peers):
    barrier = pltpu.get_barrier_semaphore()
    for peer in peers:
        pl.semaphore_signal(barrier, inc=1, device_id=peer, device_id_type=MESH)
    pl.semaphore_wait(barrier, len(peers))


def spread_blocks(n, me, buf, send, near, far, passed):
    sibling = me + 1 - 2 * lax.rem(me, 2)

    def copy(slot, to, s, recv):
        return pltpu.make_async_remote_copy(
            src_ref=buf.at[slot], dst_ref=buf.at[slot], send_sem=send.at[s], recv_sem=recv,
            device_id=at_resp(to), device_id_type=MESH,
        )

    hops = n // 2
    out = [copy(me, lax.rem(me + 2 * k, n), k, far.at[k]) for k in range(1, hops)]
    own = copy(me, sibling, 0, near.at[0])
    for c in out:
        c.start()
    own.start()
    handed = []
    for k in range(1, hops):
        out[k - 1].wait_recv()
        c = copy(lax.rem(me - 2 * k + n, n), sibling, hops + k - 1, passed.at[k])
        c.start()
        handed.append(c)
    own.wait()
    for c in out:
        c.wait_send()
    for c in handed:
        c.wait()


def gather_kernel(n, mine_ref, all_ref, send, near, far, passed):
    me = lax.axis_index("resp")
    sibling = me + 1 - 2 * lax.rem(me, 2)
    greet([at_resp(lax.rem(me + 2 * k, n)) for k in range(1, n // 2)] + [at_resp(sibling)])
    all_ref[me] = mine_ref[...]
    spread_blocks(n, me, all_ref, send, near, far, passed)


def spread_scratch(n):
    return [
        pltpu.SemaphoreType.DMA((n,)),
        pltpu.SemaphoreType.DMA((1,)),
        pltpu.SemaphoreType.DMA((n // 2,)),
        pltpu.SemaphoreType.DMA((n // 2,)),
    ]


VM = pl.BlockSpec(memory_space=pltpu.VMEM)


def gather_blocks(n, mine):
    return pl.pallas_call(
        functools.partial(gather_kernel, n),
        out_shape=jax.ShapeDtypeStruct((n,) + mine.shape, mine.dtype),
        in_specs=[VM],
        out_specs=VM,
        scratch_shapes=spread_scratch(n),
        compiler_params=pltpu.CompilerParams(
            collective_id=1, has_side_effects=True, vmem_limit_bytes=6 * 2**20
        ),
    )(mine)


CHIPS = 4
PARTS = 8


def sum_kernel(
    n, nh, dkv_ref, rows_ref, sel_ref, all_ref, lat_ref,
    got_rows, at_head, sib, mine, outer, half, other,
    s2, r2, s3, r3, ss, sr, es, er, hs, hr, ts, tr, gs, gr,
):
    me = lax.axis_index("resp")
    head = lax.axis_index("head")
    core = lax.rem(me, 2)
    z = me // 2
    sibling = me + 1 - 2 * core
    beside = 2 * (z + 1 - 2 * lax.rem(z, 2)) + core
    across = 2 * (CHIPS - 1 - z) + core
    inner = (z == 1) | (z == 2)
    peers = [lax.rem(me + k, n) for k in range(1, n)]
    heads = [lax.rem(head + k, nh) for k in range(1, nh)]
    greet([at_resp(r) for r in peers] + [(me, h) for h in heads])
    pairs = dkv_ref.shape[0] // 2
    keys = mine.shape[1]

    def copy(src, dst, s, r, i, to):
        return pltpu.make_async_remote_copy(
            src_ref=src, dst_ref=dst, send_sem=s.at[i], recv_sem=r.at[i],
            device_id=to, device_id_type=MESH,
        )

    sib_copies = [
        copy(dkv_ref.at[(1 - core) * pairs + j], sib.at[j], ss, sr, j, at_resp(sibling))
        for j in range(pairs)
    ]
    for c in sib_copies:
        c.start()
    row_copies = [
        copy(rows_ref.at[peers[k]], got_rows.at[k], s2, r2, k, at_resp(peers[k])) for k in range(n - 1)
    ]
    for c in row_copies:
        c.start()
    head_copies = [
        copy(at_head.at[head], at_head.at[head], s3, r3, k, (me, heads[k])) for k in range(nh - 1)
    ]
    inwards = [copy(mine.at[i], outer.at[i], es, er, i, at_resp(beside)) for i in range(PARTS)]
    middle = [copy(half.at[i], other.at[i], hs, hr, i, at_resp(across)) for i in range(PARTS)]
    slots = [all_ref.at[core * PARTS + i] for i in range(PARTS)]
    outwards = [copy(slots[i], slots[i], ts, tr, i, at_resp(beside)) for i in range(PARTS)]
    shared = [copy(slots[i], slots[i], gs, gr, i, at_resp(sibling)) for i in range(PARTS)]

    def chip_terms(j):
        sib_copies[j].wait_recv()
        total = dot_nn(sel_ref[me], dkv_ref[core * pairs + j]) + dot_nn(sel_ref[sibling], sib[j])
        mine[2 * j] = total[:keys].astype(BF)
        mine[2 * j + 1] = total[keys:].astype(BF)

    def sum_rows():
        rows = rows_ref[me].astype(F32)
        for k in range(n - 1):
            row_copies[k].wait_recv()
            rows = rows + got_rows[k].astype(F32)
        at_head[head] = rows
        for c in head_copies:
            c.start()

    def finish(i):
        middle[i].wait_recv()
        all_ref[core * PARTS + i] = (half[i].astype(F32) + other[i].astype(F32)).astype(BF)
        outwards[i].start()
        shared[i].start()

    @pl.when(inner)
    def _():
        for j in range(pairs):
            chip_terms(j)
        for i in range(PARTS):
            inwards[i].wait_recv()
            half[i] = (mine[i].astype(F32) + outer[i].astype(F32)).astype(BF)
            middle[i].start()
            if i >= 1:
                finish(i - 1)
            if i == PARTS // 2:
                sum_rows()
        finish(PARTS - 1)
        for i in range(PARTS):
            middle[i].wait_send()
            outwards[i].wait_send()

    @pl.when(jnp.logical_not(inner))
    def _():
        for j in range(pairs):
            chip_terms(j)
            inwards[2 * j].start()
            inwards[2 * j + 1].start()
        sum_rows()
        for i in range(PARTS):
            outwards[i].wait_recv()
            shared[i].start()
        for i in range(PARTS):
            inwards[i].wait_send()

    for c in head_copies:
        c.wait()
    lat = at_head[0]
    for h in range(1, nh):
        lat = lat + at_head[h]
    lat_ref[...] = lat
    for c in shared:
        c.wait()
    for c in row_copies + sib_copies:
        c.wait_send()


def sum_parts(n, nh, dkv, rows, select):
    pairs, keys, wide = dkv.shape
    dma = lambda k: pltpu.SemaphoreType.DMA((k,))
    part = pltpu.VMEM((PARTS, select.shape[1] // 2, wide), BF)
    summed, lat = pl.pallas_call(
        functools.partial(sum_kernel, n, nh),
        out_shape=[
            jax.ShapeDtypeStruct((2 * pairs, select.shape[1] // 2, wide), BF),
            jax.ShapeDtypeStruct(rows.shape[1:], F32),
        ],
        in_specs=[VM] * 3,
        out_specs=[VM] * 2,
        scratch_shapes=[
            pltpu.VMEM((n - 1,) + rows.shape[1:], BF),
            pltpu.VMEM((nh,) + rows.shape[1:], F32),
            pltpu.VMEM((pairs // 2, keys, wide), BF),
            part, part, part, part,
            dma(n - 1), dma(n - 1), dma(nh - 1), dma(nh - 1), dma(pairs // 2), dma(pairs // 2),
        ] + [dma(PARTS)] * 8,
        compiler_params=pltpu.CompilerParams(
            collective_id=2, has_side_effects=True, vmem_limit_bytes=32 * 2**20
        ),
    )(dkv, rows, select)
    return summed.reshape(pairs, select.shape[1], wide), lat


def weights_kernel(sum_ref, lat_ref, duk_ref, duv_ref, lat_t):
    @pl.when(pl.program_id(0) == 0)
    def _():
        lat_t[...] = lat_ref[...].T

    lat = lat_ref[...]
    for pair in range(STEP // 2):
        for i in range(2):
            at = 2 * i * HD
            duk_ref[2 * pair + i] = dot_tn(sum_ref[pair, :, at:at + HD], lat).astype(BF)
            duv_ref[2 * pair + i] = dot_nn(
                lat_t[...], sum_ref[pair, :, at + HD:at + 2 * HD]
            ).astype(BF)


def weight_grads(summed, lat_all):
    pairs, rows, wide = summed.shape
    return pl.pallas_call(
        weights_kernel,
        grid=(2 * pairs // STEP,),
        in_specs=[
            pl.BlockSpec((STEP // 2, rows, wide), lambda i: (i, 0, 0)),
            pl.BlockSpec((rows, LAT), lambda i: (0, 0)),
        ],
        out_specs=[
            pl.BlockSpec((STEP, HD, LAT), lambda i: (i, 0, 0)),
            pl.BlockSpec((STEP, LAT, HD), lambda i: (i, 0, 0)),
        ],
        out_shape=[
            jax.ShapeDtypeStruct((2 * pairs, HD, LAT), BF),
            jax.ShapeDtypeStruct((2 * pairs, LAT, HD), BF),
        ],
        scratch_shapes=[pltpu.VMEM((LAT, rows), BF)],
        compiler_params=pltpu.CompilerParams(vmem_limit_bytes=32 * 2**20),
    )(summed, lat_all)


def per_device(
    n, nh, q_nope, q_rope, latents, w_uk, w_uv, grad_out, prompt_of, live_rows, prompt_block
):
    pairs = w_uk.shape[0] // 2
    held = latents.shape[0]
    stretches = prompt_of.shape[1]
    blocks = prompt_block[prompt_of[0]]
    ids = jnp.zeros((ID_ROWS, LAT + ROPE), BF).at[0, :stretches].set(blocks.astype(BF))
    gathered = gather_blocks(n, jnp.concatenate([latents, ids], axis=0))
    table = gathered[:, :held].reshape(n * held, LAT + ROPE)
    all_blocks = gathered[:, held, :stretches].astype(jnp.int32)
    rows = n * held
    keys = jnp.take(
        table.reshape(rows // P_SIZE, P_SIZE, LAT + ROPE), blocks, axis=0
    ).reshape(-1, LAT + ROPE)
    d_nope, d_rope, dkv, d_keys = local_part(
        live_rows[0], q_nope, q_rope, grad_out, w_uk, w_uv, keys
    )

    def rows_of(which):
        at = which[..., :, None] * P_SIZE + jnp.arange(P_SIZE)
        at = at.reshape(which.shape[:-1] + (-1,))
        return jnp.arange(rows)[:, None] == at[..., None, :]

    select = rows_of(blocks)
    partial_rows = jnp.dot(select.astype(F32), d_keys, precision=lax.Precision.HIGHEST)
    if pairs == n == 2 * CHIPS:
        summed, grad_lat = sum_parts(
            n, nh, dkv, partial_rows.astype(BF).reshape(n, held, LAT + ROPE),
            rows_of(all_blocks).astype(BF),
        )
    else:
        holder_rows = lax.psum_scatter(partial_rows, "resp", scatter_dimension=0, tiled=True)
        grad_lat = lax.psum(holder_rows, "head")
        spread = jnp.einsum("nk,ukd->und", select.astype(BF), dkv, preferred_element_type=F32)
        summed = lax.psum(spread, "resp").astype(BF)
    final_uk, final_uv = weight_grads(summed, table[:, :LAT])
    return d_nope, d_rope, grad_lat, final_uk, final_uv


def solution(mesh):
    in_specs = (
        P("resp", "head"),
        P("resp", "head"),
        P("resp", None),
        P("head", None, None),
        P("head", None, None),
        P("resp", "head"),
        P("resp", None),
        P("resp", None),
        P(),
    )
    out_specs = (
        P("resp", "head"),
        P("resp", "head"),
        P("resp", None),
        P("head", None, None),
        P("head", None, None),
    )
    return jax.shard_map(
        functools.partial(per_device, mesh.shape["resp"], mesh.shape["head"]), mesh=mesh, in_specs=in_specs, out_specs=out_specs, check_vma=False
    )
```
